128 devices in a mesh: section: 32 (over z, x_hi, y), tensor: 4 (over x_lo, core).
Axes of the slice: x: 4 (x_hi: 2, x_lo: 2; x = x_hi * 2 + x_lo), y: 4, z: 4, core: 2. Of those that a mesh axis runs over, the one named last changes fastest.
Arguments:
- act: bfloat16 [32, 1024, 2048], P('section', 'tensor'), may hold values from -6 to 6
- group_of: int32 [32], P('section'), may hold values from 0 to 1, as said below
- gain: bfloat16 [32, 2, 2048], P('section'), may hold values from 0.5 to 1.5
- w_in: bfloat16 [32, 2, 2048, 4096], P('section', None, None, 'tensor'), may hold values from -0.125 to 0.125
- w_out: bfloat16 [32, 2, 4096, 2048], P('section', None, 'tensor'), may hold values from -0.09375 to 0.09375
Outputs:
- next_act: bfloat16 [32, 1024, 2048], P('section', 'tensor')
- parked: bfloat16 [32, 1024, 2048], P('section', 'tensor')
The draws below stay inside these ranges and needn't reach their ends.
Inputs may be any that keep to these rules, and one draw needn't show every extreme that they name: `group_of`: every entry is 0 or 1; the entry of the last section is 0.
All inputs are finite; a program needn't handle non-finite values.
Results may differ from the reference program's by a relative error of at most 0.017.
Values may be sent and summed in bfloat16 or wider, within the bound.
No kernel may reach another device: no remote copies, remote signals or barrier semaphores. Data moves between devices by JAX's collectives and lax.ppermute only.
A program may use at most 128 MiB of HBM per device.

```python
import jax
import jax.numpy as jnp
from jax import lax

D = 2048
HID = 4096
TOK = 1024
GROUPS = 2
SECTIONS = 32
HID_DEV = 1024
N_TENSOR = 4


def draw_group_of(key, part):
    key = jax.random.fold_in(key, 7)
    drawn = jax.random.randint(key, (SECTIONS,), 0, 2, dtype=jnp.int32)
    return drawn.at[SECTIONS - 1].set(0)


def block_levels(key, dims, split, least, high):
    factor_of = 1.0
    for dim, blocks in split:
        steps = jax.random.uniform(jax.random.fold_in(jax.random.fold_in(key, 6), dim), (blocks,), jnp.float32, least / len(split), high / len(split))
        factor_of = factor_of * jnp.repeat(jnp.exp(steps), dims[dim] // blocks).reshape((-1,) + (1,) * (len(dims) - 1 - dim))
    return factor_of


def normal_values(key, shape, width, reach, split=(), held_as=jnp.bfloat16):
    level = block_levels(key, shape, split, -0.22, 0.18) if split else 1.0
    array = jax.random.normal(key, shape, jnp.float32) * width * level
    return jnp.minimum(jnp.maximum(array, -reach), reach).astype(held_as)


def setup_inputs(seed: int = 0) -> dict:
    key_list = jax.random.split(jax.random.key(seed), 6)
    return {
        "act": normal_values(key_list[0], (SECTIONS, TOK, D), 1.0, 6.0, ((0, 32), (1, 4))),
        "group_of": draw_group_of(jax.random.fold_in(key_list[5], 71), 0),
        "gain": jnp.clip(1.0 + 0.1 * jax.random.normal(key_list[2], (SECTIONS, GROUPS, D), jnp.float32), 0.5, 1.5).astype(jnp.bfloat16),
        "w_in": normal_values(key_list[3], (SECTIONS, GROUPS, D, HID), D ** -0.5, 0.125, ((0, 32), (3, 4))),
        "w_out": normal_values(key_list[4], (SECTIONS, GROUPS, HID, D), HID ** -0.5, 0.09375, ((0, 32), (2, 4))),
    }


eps = 1e-05

def normalize(row_block, gain_row):
    as_float = row_block.astype(jnp.float32)
    centred = as_float - lax.optimization_barrier(jnp.mean(as_float, axis=-1, keepdims=True))
    spread = lax.optimization_barrier(jnp.mean(centred * centred, axis=-1, keepdims=True))
    return (centred * lax.rsqrt(spread + eps) * gain_row.astype(jnp.float32)).astype(jnp.bfloat16)

def apply_layer(row_block, gain_row, w_first, w_second):
    normed = normalize(row_block, gain_row)
    hidden = jax.nn.gelu(jnp.dot(normed, w_first, preferred_element_type=jnp.float32), approximate=True).astype(jnp.bfloat16)
    summed = jnp.zeros(row_block.shape, jnp.float32)
    for column_part in range(N_TENSOR):
        low = column_part * HID_DEV
        partial_value = jnp.dot(hidden[:, low:low + HID_DEV], w_second[low:low + HID_DEV], preferred_element_type=jnp.float32)
        rounded = lax.optimization_barrier(partial_value.astype(jnp.bfloat16))
        summed = summed + rounded.astype(jnp.float32)
    return (row_block.astype(jnp.float32) + summed).astype(jnp.bfloat16)

def reference(act, group_of, gain, w_in, w_out):
    section_ids = jnp.arange(SECTIONS, dtype=jnp.int32)

    def run_sections(inputs, group_table):

        def single(section_id):
            group_id = group_table[section_id]
            return apply_layer(inputs[section_id], gain[section_id, group_id], w_in[section_id, group_id], w_out[section_id, group_id])
        return lax.map(single, section_ids)
    first = run_sections(act, group_of)
    arrived = jnp.roll(first, 1, axis=0)
    group_two = jnp.roll(group_of, 1).at[0].set(1)
    next_act = run_sections(arrived, group_two)
    parked = arrived[::-1]
    return (next_act, parked)
```

```python
import functools

import jax
import jax.numpy as jnp
from jax import lax
from jax.experimental import pallas as pl
from jax.experimental.pallas import tpu as pltpu
from jax.sharding import PartitionSpec as P

eps = 1e-05
AXES = ("section", "tensor")
Y = 4
CHUNKS = (64, 64, 64, 64)
HB = 512
VMEM_LIMIT = 8 * 2**20


def route(x, to):
    sections, tensors = (lax.axis_size(a) for a in AXES)
    pairs = []
    for s in range(sections):
        for t in range(tensors):
            ds, dt = to(s, t, sections)
            pairs.append((s * tensors + t, ds * tensors + dt))
    return lax.ppermute(x, AXES, pairs)


def to_x_neighbour(s, t, n):
    return s, t ^ 2


def to_other_core(s, t, n):
    return s, t ^ 1


def to_next_section(s, t, n):
    return (s + 1) % n, (t ^ 2 if s % Y == Y - 1 else t)


def to_next_plain(s, t, n):
    return (s + 1) % n, t


def to_mirror(s, t, n):
    return n - 1 - s, t ^ 2


def pick_kernel(idx, w_in, w_out, in_sel, out_sel, sems):
    g = idx[0]
    parts = 4
    copies = []
    for k in range(parts):
        a = w_in.shape[2] // parts
        b = w_out.shape[2] // parts
        copies.append(pltpu.make_async_copy(w_in.at[0, g, pl.ds(k * a, a)], in_sel.at[pl.ds(k * a, a)], sems.at[2 * k]))
        copies.append(pltpu.make_async_copy(w_out.at[0, g, pl.ds(k * b, b)], out_sel.at[pl.ds(k * b, b)], sems.at[2 * k + 1]))
    for c in copies:
        c.start()
    for c in copies:
        c.wait()


def in_vmem(x):
    return pltpu.with_memory_space_constraint(x, pltpu.VMEM)


def in_hbm(x):
    return pltpu.with_memory_space_constraint(x, pltpu.HBM)


def pick(group, w_in, w_out):
    hbm = pl.BlockSpec(memory_space=pltpu.HBM)
    vmem = pl.BlockSpec(memory_space=pltpu.VMEM)
    return pl.pallas_call(
        pick_kernel,
        out_shape=(
            pltpu.VMEM(w_in.shape[2:], w_in.dtype),
            pltpu.VMEM(w_out.shape[2:], w_out.dtype),
        ),
        in_specs=[pl.BlockSpec(memory_space=pltpu.SMEM), hbm, hbm],
        out_specs=(vmem, vmem),
        scratch_shapes=[pltpu.SemaphoreType.DMA((8,))],
        compiler_params=pltpu.CompilerParams(vmem_limit_bytes=2**20),
        cost_estimate=pl.CostEstimate(flops=0, bytes_accessed=8 * 2**20, transcendentals=0),
        name="pick_group",
    )(group.reshape(1), in_hbm(w_in), in_hbm(w_out))


def block_kernel(idx, own, par, gain, w_in, w_out, r_in, r_out, *refs):
    give, keep, normed, total = refs[-4:]
    g, swap = idx[0], idx[1]
    rows = own.shape[0]
    per = r_in.shape[1] // HB
    swapped = swap == 1
    gain_row = jnp.where(g == 0, gain[0, 0:1, :], gain[0, 1:2, :]).astype(jnp.float32)
    x_own = own[...].astype(jnp.float32)
    x_par = par[...].astype(jnp.float32)
    x_keep = jnp.where(swapped, x_par, x_own)
    x_give = jnp.where(swapped, x_own, x_par)
    for k, x in enumerate((x_keep, x_give)):
        centred = x - jnp.mean(x, axis=-1, keepdims=True)
        spread = jnp.mean(centred * centred, axis=-1, keepdims=True)
        normed[pl.ds(k * rows, rows), :] = (centred * lax.rsqrt(spread + eps) * gain_row).astype(jnp.bfloat16)
    for b in range(2 * per):
        first, second = (w_in, w_out) if b < per else (r_in, r_out)
        lo = (b % per) * HB
        up = jnp.dot(normed[...], first[:, pl.ds(lo, HB)], preferred_element_type=jnp.float32)
        hidden = jax.nn.gelu(up, approximate=True).astype(jnp.bfloat16)
        part = jnp.dot(hidden, second[pl.ds(lo, HB), :], preferred_element_type=jnp.float32)
        if b == 0:
            total[...] = part
        elif b < 2 * per - 1:
            total[...] += part
        else:
            give[...] = (total[pl.ds(rows, rows), :] + part[rows:]).astype(jnp.bfloat16)
            kept = jnp.where(swapped, par[...].astype(jnp.float32), own[...].astype(jnp.float32))
            keep[...] = kept + (total[pl.ds(0, rows), :] + part[:rows])


def block(idx, own, par, gain, w_in, w_out, r_in, r_out, *behind):
    rows, d = own.shape
    hid = r_in.shape[1]
    vmem = pl.BlockSpec(memory_space=pltpu.VMEM)
    return pl.pallas_call(
        block_kernel,
        out_shape=(
            jax.ShapeDtypeStruct((rows, d), jnp.bfloat16),
            jax.ShapeDtypeStruct((rows, d), jnp.float32),
        ),
        in_specs=[pl.BlockSpec(memory_space=pltpu.SMEM)] + [vmem] * 7 + [pl.BlockSpec(memory_space=pl.ANY)] * len(behind),
        out_specs=(vmem, vmem),
        scratch_shapes=[
            pltpu.VMEM((2 * rows, d), jnp.bfloat16),
            pltpu.VMEM((2 * rows, d), jnp.float32),
        ],
        compiler_params=pltpu.CompilerParams(vmem_limit_bytes=VMEM_LIMIT),
        cost_estimate=pl.CostEstimate(
            flops=2 * 2 * (2 * rows) * d * 2 * hid, bytes_accessed=4 * 2 * hid * d, transcendentals=2 * rows * 2 * hid
        ),
        name="block",
    )(idx, own, par, gain, *(in_vmem(w) for w in (w_in, w_out, r_in, r_out)), *behind)


def join_kernel(keep, got, *refs):
    refs[-1][...] = (keep[...] + got[...].astype(jnp.float32)).astype(jnp.bfloat16)


def join(keep, got, *behind):
    vmem = pl.BlockSpec(memory_space=pltpu.VMEM)
    return pl.pallas_call(
        join_kernel,
        out_shape=jax.ShapeDtypeStruct(got.shape, jnp.bfloat16),
        in_specs=[vmem, vmem] + [pl.BlockSpec(memory_space=pl.ANY)] * len(behind),
        out_specs=vmem,
        compiler_params=pltpu.CompilerParams(vmem_limit_bytes=4 * 2**20),
        cost_estimate=pl.CostEstimate(flops=got.size, bytes_accessed=8 * got.size, transcendentals=0),
        name="join",
    )(keep, got, *behind)


def body(act, group_of, gain, w_in, w_out):
    place = lax.axis_index("section")
    g1 = group_of[0]
    prior = route(group_of, to_next_plain)[0]
    g2 = jnp.where(place == 0, 1, prior).astype(jnp.int32)
    swap = (place % Y == Y - 1).astype(jnp.int32)
    none = jnp.zeros((), jnp.int32)
    starts = [sum(CHUNKS[:k]) for k in range(len(CHUNKS))]

    own1 = [act[0, lo : lo + n] for lo, n in zip(starts, CHUNKS)]
    par1 = [route(x, to_x_neighbour) for x in own1]
    r_in, r_out = route(w_in, to_other_core), route(w_out, to_other_core)
    w1 = pick(g1, w_in, w_out) + pick(g1, r_in, r_out)
    w2 = pick(g2, w_in, w_out) + pick(g2, r_in, r_out)

    idx1, idx2 = jnp.stack([g1, swap, g2]), jnp.stack([g2, none, none])
    last = len(CHUNKS) - 1

    own2 = []
    for k, (x, y) in enumerate(zip(own1, par1)):
        give, keep = block(idx1, x, y, gain, *w1)
        behind = w2 if k == last else ()
        own2.append(route(join(keep, route(give, to_x_neighbour), *behind), to_next_section))

    halves, parked = [], []
    for k, x in enumerate(own2):
        y = route(x, to_x_neighbour)
        parked.append(route(y, to_mirror))
        give, keep = block(idx2, x, y, gain, *w2, *parked[: max(k - 1, 0)][-1:])
        halves.append((keep, route(give, to_x_neighbour)))
    outs = [join(*halves[k], *parked[k + last - 1 :][:1]) for k in range(len(halves))]
    return jnp.concatenate(outs)[None], jnp.concatenate(parked)[None]


def solution(mesh):
    placed = (
        P("section", "tensor", None),
        P("section"),
        P("section", None, None),
        P("section", None, None, "tensor"),
        P("section", None, "tensor", None),
    )
    return jax.shard_map(
        body,
        mesh=mesh,
        in_specs=placed,
        out_specs=(P("section", "tensor", None), P("section", "tensor", None)),
        check_vma=False,
    )
```

```python
import functools

import jax
import jax.numpy as jnp
from jax import lax
from jax.experimental import pallas as pl
from jax.experimental.pallas import tpu as pltpu
from jax.sharding import PartitionSpec as P

eps = 1e-05
AXES = ("section", "tensor")
Y = 4
HB = 512
MIB = 2**20
ROWS = 64


def route(x, to):
    sections, tensors = (lax.axis_size(a) for a in AXES)
    pairs = []
    for s in range(sections):
        for t in range(tensors):
            ds, dt = to(s, t, sections)
            pairs.append((s * tensors + t, ds * tensors + dt))
    return lax.ppermute(x, AXES, pairs)


def to_x_neighbour(s, t, n):
    return s, t ^ 2


def to_other_core(s, t, n):
    return s, t ^ 1


def to_next_section(s, t, n):
    return (s + 1) % n, (t ^ 2 if s % Y == Y - 1 else t)


def to_mirror(s, t, n):
    return n - 1 - s, t ^ 2


def in_vmem(x):
    return pltpu.with_memory_space_constraint(x, pltpu.VMEM)


def in_hbm(x):
    return pltpu.with_memory_space_constraint(x, pltpu.HBM)


class Order:
    def __init__(self):
        self.token = jnp.zeros((8, 128), jnp.float32)

    def call(self, kernel, name, outs, specs, args, scratch=(), vmem=4 * MIB, us=0.1, behind=()):
        vmem_spec = pl.BlockSpec(memory_space=pltpu.VMEM)

        def with_token(*refs):
            ins = refs[: len(args)]
            rest = refs[len(args) + 1 + len(behind) :]
            rest[len(outs)][...] = jnp.zeros((8, 128), jnp.float32)
            kernel(*ins, *rest[: len(outs)], *rest[len(outs) + 1 :])

        *results, self.token = pl.pallas_call(
            with_token,
            out_shape=tuple(outs) + (jax.ShapeDtypeStruct((8, 128), jnp.float32),),
            in_specs=list(specs) + [pl.BlockSpec(memory_space=pl.ANY)] * (1 + len(behind)),
            out_specs=(vmem_spec,) * (len(outs) + 1),
            scratch_shapes=list(scratch),
            compiler_params=pltpu.CompilerParams(vmem_limit_bytes=vmem),
            cost_estimate=pl.CostEstimate(flops=int(us * 1.15e9), bytes_accessed=2**14, transcendentals=0),
            name=name,
        )(*args, self.token, *behind)
        return results


SMEM_SPEC = pl.BlockSpec(memory_space=pltpu.SMEM)
VMEM_SPEC = pl.BlockSpec(memory_space=pltpu.VMEM)
HBM_SPEC = pl.BlockSpec(memory_space=pltpu.HBM)


def pick_kernel(groups, count, idx, *refs):
    ws, outs, sems = refs[:count], refs[count : (1 + groups) * count], refs[(1 + groups) * count]
    loads = []
    for j in range(groups):
        for n in range(count):
            for k in range(4):
                size = ws[n].shape[2] // 4
                piece = pl.ds(k * size, size)
                held = outs[j * count + n]
                loads.append(pltpu.make_async_copy(ws[n].at[0, idx[j], piece], held.at[piece], sems.at[len(loads)]))
    for load in loads:
        load.start()
    for load in loads:
        load.wait()


def pick(order, groups, ws, behind=()):
    n = len(ws)
    held = order.call(
        functools.partial(pick_kernel, len(groups), n),
        "pick_group",
        [pltpu.VMEM(w.shape[2:], w.dtype) for w in ws] * len(groups),
        [SMEM_SPEC] + [HBM_SPEC] * n,
        (jnp.stack(groups), *(in_hbm(w) for w in ws)),
        [pltpu.SemaphoreType.DMA((4 * n * len(groups),))],
        us=1.7 * n * len(groups),
        behind=behind,
    )
    return [held[j * n : (j + 1) * n] for j in range(len(groups))]


def normalize(x, gain_row):
    centred = x - jnp.mean(x, axis=-1, keepdims=True)
    spread = jnp.mean(centred * centred, axis=-1, keepdims=True)
    return (centred * lax.rsqrt(spread + eps) * gain_row).astype(jnp.bfloat16)


def up(normed, w):
    return jax.nn.gelu(jnp.dot(normed, w, preferred_element_type=jnp.float32), approximate=True).astype(jnp.bfloat16)


def prepare(idx, own, par, gain, normed):
    rows = own.shape[0]
    swapped = idx[1] == 1
    gain_row = jnp.where(idx[0] == 0, gain[0, 0:1, :], gain[0, 1:2, :]).astype(jnp.float32)
    x_own = own[...].astype(jnp.float32)
    x_par = par[...].astype(jnp.float32)
    normed[pl.ds(0, rows), :] = normalize(jnp.where(swapped, x_par, x_own), gain_row)
    normed[pl.ds(rows, rows), :] = normalize(jnp.where(swapped, x_own, x_par), gain_row)


def kept_rows(idx, own, par):
    return jnp.where(idx[1] == 1, par[...].astype(jnp.float32), own[...].astype(jnp.float32))


def window(ref, lo, rows):
    return ref.at[pl.ds(lo, rows)]


def block_kernel(own_lo, par_lo, idx, own, par, gain, w_in, w_out, r_in, r_out, give, keep, normed, total):
    rows = give.shape[0]
    own, par = window(own, own_lo, rows), window(par, par_lo, rows)
    prepare(idx, own, par, gain, normed)
    per = r_in.shape[1] // HB
    for b in range(2 * per):
        first, second = (w_in, w_out) if b < per else (r_in, r_out)
        piece = pl.ds((b % per) * HB, HB)
        part = jnp.dot(up(normed[...], first[:, piece]), second[piece, :], preferred_element_type=jnp.float32)
        if b == 0:
            total[...] = part
        elif b < 2 * per - 1:
            total[...] += part
        else:
            give[...] = (total[pl.ds(rows, rows), :] + part[rows:]).astype(jnp.bfloat16)
            keep[...] = kept_rows(idx, own, par) + (total[pl.ds(0, rows), :] + part[:rows])


def block(order, idx, own, par, gain, ws, own_lo=0, par_lo=0, behind=()):
    d = own.shape[1]
    return order.call(
        functools.partial(block_kernel, own_lo, par_lo),
        "block",
        [jax.ShapeDtypeStruct((ROWS, d), jnp.bfloat16), jax.ShapeDtypeStruct((ROWS, d), jnp.float32)],
        [SMEM_SPEC] + [VMEM_SPEC] * 7,
        (idx, own, par, gain, *(in_vmem(w) for w in ws)),
        [pltpu.VMEM((2 * ROWS, d), jnp.bfloat16), pltpu.VMEM((2 * ROWS, d), jnp.float32)],
        8 * MIB,
        us=4,
        behind=behind,
    )


def up_kernel(idx, own, par, gain, w_in, r_in, hidden, normed):
    for k in range(own.shape[0] // ROWS):
        prepare(idx, window(own, k * ROWS, ROWS), window(par, k * ROWS, ROWS), gain, window(normed, 2 * k * ROWS, 2 * ROWS))
    units = w_in.shape[1]
    for n, w in enumerate((w_in, r_in)):
        for lo in range(0, units, HB):
            hidden[:, pl.ds(n * units + lo, HB)] = up(normed[...], w[:, pl.ds(lo, HB)])


def up_rows(order, idx, own, par, gain, w_in, r_in):
    rows, d = own.shape
    return order.call(
        up_kernel,
        "up",
        [jax.ShapeDtypeStruct((2 * rows, 2 * w_in.shape[1]), jnp.bfloat16)],
        [SMEM_SPEC] + [VMEM_SPEC] * 5,
        (idx, own, par, gain, in_vmem(w_in), in_vmem(r_in)),
        [pltpu.VMEM((2 * rows, d), jnp.bfloat16)],
        8 * MIB,
        us=3,
    )[0]


def down_kernel(lo, idx, own, par, hidden, w_out, r_out, give, keep):
    rows = give.shape[0]
    units = w_out.shape[0]
    mine = window(hidden, 2 * lo, 2 * rows)
    total = jnp.dot(mine[:, pl.ds(0, units)], w_out[...], preferred_element_type=jnp.float32)
    total += jnp.dot(mine[:, pl.ds(units, units)], r_out[...], preferred_element_type=jnp.float32)
    give[...] = total[rows:].astype(jnp.bfloat16)
    keep[...] = kept_rows(idx, window(own, lo, rows), window(par, lo, rows)) + total[:rows]


def down(order, idx, own, par, hidden, w_out, r_out, lo, behind=()):
    d = own.shape[1]
    return order.call(
        functools.partial(down_kernel, lo),
        "down",
        [jax.ShapeDtypeStruct((ROWS, d), jnp.bfloat16), jax.ShapeDtypeStruct((ROWS, d), jnp.float32)],
        [SMEM_SPEC] + [VMEM_SPEC] * 5,
        (idx, own, par, hidden, in_vmem(w_out), in_vmem(r_out)),
        vmem=8 * MIB,
        us=2,
        behind=behind,
    )


def join_kernel(keep, got, out):
    out[...] = (keep[...] + got[...].astype(jnp.float32)).astype(jnp.bfloat16)


def join(order, keep, got, behind=()):
    shape = jax.ShapeDtypeStruct(got.shape, jnp.bfloat16)
    return order.call(join_kernel, "join", [shape], [VMEM_SPEC] * 2, (keep, got), us=0.5, behind=behind)[0]


def last_kernel(keep, got, *refs):
    *done, out = refs
    rows = keep.shape[0]
    for k, x in enumerate(done):
        out[0, pl.ds(k * rows, rows), :] = x[...]
    out[0, pl.ds(len(done) * rows, rows), :] = (keep[...] + got[...].astype(jnp.float32)).astype(jnp.bfloat16)


def pack_kernel(*refs):
    *xs, out = refs
    rows = xs[0].shape[0]
    for k, x in enumerate(xs):
        out[0, pl.ds(k * rows, rows), :] = x[...]


def whole(order, kernel, name, args, rows):
    shape = jax.ShapeDtypeStruct((1, rows, args[0].shape[1]), jnp.bfloat16)
    return order.call(kernel, name, [shape], [VMEM_SPEC] * len(args), args, vmem=8 * MIB, us=0.5)[0]


def body(act, group_of, gain, w_in, w_out):
    place = lax.axis_index("section")
    g1 = group_of[0]
    prior = route(group_of, to_next_section)[0]
    g2 = jnp.where(place == 0, 1, prior).astype(jnp.int32)
    swap = (place % Y != Y - 1).astype(jnp.int32)
    idx1, idx2 = jnp.stack([g1, swap]), jnp.stack([g2, jnp.ones((), jnp.int32)])
    order = Order()

    def across(x):
        return route(x, to_x_neighbour)

    def onward(x):
        return route(x, to_next_section)

    def mirror(*xs):
        return route(whole(order, pack_kernel, "pack", xs, len(xs) * ROWS), to_mirror)

    rows = act.shape[1]
    r_in, r_out = route(w_in, to_other_core), route(w_out, to_other_core)
    own = [act[0, : rows // 2], act[0, rows // 2 :]]
    par = [across(x) for x in own]

    ((w_in1, w_out1, r_in1),) = pick(order, (g1,), (w_in, w_out, r_in))
    hidden = up_rows(order, idx1, own[0], par[0], gain, w_in1, r_in1)
    ((r_out1,),) = pick(order, (g1,), (r_out,))
    w1 = (w_in1, w_out1, r_in1, r_out1)
    give, keep0 = down(order, idx1, own[0], par[0], hidden, w_out1, r_out1, 0)
    got0 = across(give)
    give, keep1 = down(order, idx1, own[0], par[0], hidden, w_out1, r_out1, ROWS, (par[1], g2.reshape(1)))
    got1 = across(give)
    give, keep2 = block(order, idx1, own[1], par[1], gain, w1, 0, 0)
    got2 = across(give)
    x0 = onward(join(order, keep0, got0))
    give, keep3 = block(order, idx1, own[1], par[1], gain, w1, ROWS, ROWS)
    got3 = across(give)
    x1 = onward(join(order, keep1, got1))
    ((w_in2, w_out2),) = pick(order, (g2,), (w_in, w_out))
    x2 = onward(join(order, keep2, got2))
    ((r_in2, r_out2),) = pick(order, (g2,), (r_in, r_out), (x0,))
    x3 = onward(join(order, keep3, got3, (x1,)))
    w2 = (w_in2, w_out2, r_in2, r_out2)

    y0, y1, y2, y3 = (across(x) for x in (x0, x1, x2, x3))
    give, keep0 = block(order, idx2, x0, y0, gain, w2)
    got0 = across(give)
    low = mirror(x0, x1)
    give, keep1 = block(order, idx2, x1, y1, gain, w2, behind=(x2,))
    got1 = across(give)
    high = mirror(x2, x3)
    give, keep2 = block(order, idx2, x2, y2, gain, w2, behind=(y3,))
    got2 = across(give)
    give, keep3 = block(order, idx2, x3, y3, gain, w2)
    got3 = across(give)
    done = [join(order, keep0, got0), join(order, keep1, got1, (low,)), join(order, keep2, got2)]
    stash = whole(order, pack_kernel, "pack", (low[0], high[0]), rows)
    return whole(order, last_kernel, "last", (keep3, got3, *done), rows), stash


def solution(mesh):
    placed = (
        P("section", "tensor", None),
        P("section"),
        P("section", None, None),
        P("section", None, None, "tensor"),
        P("section", None, "tensor", None),
    )
    return jax.shard_map(
        body,
        mesh=mesh,
        in_specs=placed,
        out_specs=(P("section", "tensor", None), P("section", "tensor", None)),
        check_vma=False,
    )
```

```python
import functools

import jax
import jax.numpy as jnp
from jax import lax
from jax.experimental import pallas as pl
from jax.experimental.pallas import tpu as pltpu
from jax.sharding import PartitionSpec as P

eps = 1e-05
AXES = ("section", "tensor")
Y = 4
HB = 512
MIB = 2**20
ROWS = 64


def route(x, to):
    sections, tensors = (lax.axis_size(a) for a in AXES)
    pairs = []
    for s in range(sections):
        for t in range(tensors):
            ds, dt = to(s, t, sections)
            pairs.append((s * tensors + t, ds * tensors + dt))
    return lax.ppermute(x, AXES, pairs)


def to_x_neighbour(s, t, n):
    return s, t ^ 2


def to_other_core(s, t, n):
    return s, t ^ 1


def to_next_section(s, t, n):
    return (s + 1) % n, (t ^ 2 if s % Y == Y - 1 else t)


def to_mirror(s, t, n):
    return n - 1 - s, t ^ 2


def in_vmem(x):
    return pltpu.with_memory_space_constraint(x, pltpu.VMEM)


def in_hbm(x):
    return pltpu.with_memory_space_constraint(x, pltpu.HBM)


class Order:
    def __init__(self):
        self.token = jnp.zeros((8, 128), jnp.float32)

    def call(self, kernel, name, outs, specs, args, scratch=(), vmem=4 * MIB, us=0.1, behind=()):
        vmem_spec = pl.BlockSpec(memory_space=pltpu.VMEM)

        def with_token(*refs):
            ins = refs[: len(args)]
            rest = refs[len(args) + 1 + len(behind) :]
            rest[len(outs)][...] = jnp.zeros((8, 128), jnp.float32)
            kernel(*ins, *rest[: len(outs)], *rest[len(outs) + 1 :])

        *results, self.token = pl.pallas_call(
            with_token,
            out_shape=tuple(outs) + (jax.ShapeDtypeStruct((8, 128), jnp.float32),),
            in_specs=list(specs) + [pl.BlockSpec(memory_space=pl.ANY)] * (1 + len(behind)),
            out_specs=(vmem_spec,) * (len(outs) + 1),
            scratch_shapes=list(scratch),
            compiler_params=pltpu.CompilerParams(vmem_limit_bytes=vmem),
            cost_estimate=pl.CostEstimate(flops=int(us * 1.15e9), bytes_accessed=2**14, transcendentals=0),
            name=name,
        )(*args, self.token, *behind)
        return results


SMEM_SPEC = pl.BlockSpec(memory_space=pltpu.SMEM)
VMEM_SPEC = pl.BlockSpec(memory_space=pltpu.VMEM)
HBM_SPEC = pl.BlockSpec(memory_space=pltpu.HBM)


def pick_kernel(groups, count, idx, *refs):
    ws, outs, sems = refs[:count], refs[count : (1 + groups) * count], refs[(1 + groups) * count]
    loads = []
    for j in range(groups):
        for n in range(count):
            for k in range(4):
                size = ws[n].shape[2] // 4
                piece = pl.ds(k * size, size)
                held = outs[j * count + n]
                loads.append(pltpu.make_async_copy(ws[n].at[0, idx[j], piece], held.at[piece], sems.at[len(loads)]))
    for load in loads:
        load.start()
    for load in loads:
        load.wait()


def pick(order, groups, ws, behind=()):
    n = len(ws)
    held = order.call(
        functools.partial(pick_kernel, len(groups), n),
        "pick_group",
        [pltpu.VMEM(w.shape[2:], w.dtype) for w in ws] * len(groups),
        [SMEM_SPEC] + [HBM_SPEC] * n,
        (jnp.stack(groups), *(in_hbm(w) for w in ws)),
        [pltpu.SemaphoreType.DMA((4 * n * len(groups),))],
        us=1.7 * n * len(groups),
        behind=behind,
    )
    return [held[j * n : (j + 1) * n] for j in range(len(groups))]


def normalize(x, gain_row):
    centred = x - jnp.mean(x, axis=-1, keepdims=True)
    spread = jnp.mean(centred * centred, axis=-1, keepdims=True)
    return (centred * lax.rsqrt(spread + eps) * gain_row).astype(jnp.bfloat16)


def up(normed, w):
    return jax.nn.gelu(jnp.dot(normed, w, preferred_element_type=jnp.float32), approximate=True).astype(jnp.bfloat16)


def prepare(idx, own, par, gain, normed):
    rows = own.shape[0]
    swapped = idx[1] == 1
    gain_row = jnp.where(idx[0] == 0, gain[0, 0:1, :], gain[0, 1:2, :]).astype(jnp.float32)
    x_own = own[...].astype(jnp.float32)
    x_par = par[...].astype(jnp.float32)
    normed[pl.ds(0, rows), :] = normalize(jnp.where(swapped, x_par, x_own), gain_row)
    normed[pl.ds(rows, rows), :] = normalize(jnp.where(swapped, x_own, x_par), gain_row)


def kept_rows(idx, own, par):
    return jnp.where(idx[1] == 1, par[...].astype(jnp.float32), own[...].astype(jnp.float32))


def window(ref, lo, rows):
    return ref.at[pl.ds(lo, rows)]


def block_kernel(own_lo, par_lo, idx, own, par, gain, w_in, w_out, r_in, r_out, give, keep, normed, total):
    rows = give.shape[0]
    own, par = window(own, own_lo, rows), window(par, par_lo, rows)
    prepare(idx, own, par, gain, normed)
    per = r_in.shape[1] // HB
    for b in range(2 * per):
        first, second = (w_in, w_out) if b < per else (r_in, r_out)
        piece = pl.ds((b % per) * HB, HB)
        part = jnp.dot(up(normed[...], first[:, piece]), second[piece, :], preferred_element_type=jnp.float32)
        if b == 0:
            total[...] = part
        elif b < 2 * per - 1:
            total[...] += part
        else:
            give[...] = (total[pl.ds(rows, rows), :] + part[rows:]).astype(jnp.bfloat16)
            keep[...] = kept_rows(idx, own, par) + (total[pl.ds(0, rows), :] + part[:rows])


def block(order, idx, own, par, gain, ws, own_lo=0, par_lo=0, behind=(), us=4):
    d = own.shape[1]
    return order.call(
        functools.partial(block_kernel, own_lo, par_lo),
        "block",
        [jax.ShapeDtypeStruct((ROWS, d), jnp.bfloat16), jax.ShapeDtypeStruct((ROWS, d), jnp.float32)],
        [SMEM_SPEC] + [VMEM_SPEC] * 7,
        (idx, own, par, gain, *(in_vmem(w) for w in ws)),
        [pltpu.VMEM((2 * ROWS, d), jnp.bfloat16), pltpu.VMEM((2 * ROWS, d), jnp.float32)],
        8 * MIB,
        us=us,
        behind=behind,
    )


def up_kernel(idx, own, par, gain, w_in, r_in, hidden, normed):
    for k in range(own.shape[0] // ROWS):
        prepare(idx, window(own, k * ROWS, ROWS), window(par, k * ROWS, ROWS), gain, window(normed, 2 * k * ROWS, 2 * ROWS))
    units = w_in.shape[1]
    for n, w in enumerate((w_in, r_in)):
        for lo in range(0, units, HB):
            hidden[:, pl.ds(n * units + lo, HB)] = up(normed[...], w[:, pl.ds(lo, HB)])


def up_rows(order, idx, own, par, gain, w_in, r_in):
    rows, d = own.shape
    return order.call(
        up_kernel,
        "up",
        [jax.ShapeDtypeStruct((2 * rows, 2 * w_in.shape[1]), jnp.bfloat16)],
        [SMEM_SPEC] + [VMEM_SPEC] * 5,
        (idx, own, par, gain, in_vmem(w_in), in_vmem(r_in)),
        [pltpu.VMEM((2 * rows, d), jnp.bfloat16)],
        8 * MIB,
        us=3,
    )[0]


def down_kernel(lo, idx, own, par, hidden, w_out, r_out, give, keep):
    rows = give.shape[0]
    units = w_out.shape[0]
    mine = window(hidden, 2 * lo, 2 * rows)
    total = jnp.dot(mine[:, pl.ds(0, units)], w_out[...], preferred_element_type=jnp.float32)
    total += jnp.dot(mine[:, pl.ds(units, units)], r_out[...], preferred_element_type=jnp.float32)
    give[...] = total[rows:].astype(jnp.bfloat16)
    keep[...] = kept_rows(idx, window(own, lo, rows), window(par, lo, rows)) + total[:rows]


def down(order, idx, own, par, hidden, w_out, r_out, lo, behind=()):
    d = own.shape[1]
    return order.call(
        functools.partial(down_kernel, lo),
        "down",
        [jax.ShapeDtypeStruct((ROWS, d), jnp.bfloat16), jax.ShapeDtypeStruct((ROWS, d), jnp.float32)],
        [SMEM_SPEC] + [VMEM_SPEC] * 5,
        (idx, own, par, hidden, in_vmem(w_out), in_vmem(r_out)),
        vmem=8 * MIB,
        us=2,
        behind=behind,
    )


def join_kernel(keep, got, out):
    out[...] = (keep[...] + got[...].astype(jnp.float32)).astype(jnp.bfloat16)


def join(order, keep, got, behind=(), us=0.5):
    shape = jax.ShapeDtypeStruct(got.shape, jnp.bfloat16)
    return order.call(join_kernel, "join", [shape], [VMEM_SPEC] * 2, (keep, got), us=us, behind=behind)[0]


def wait_kernel(out):
    out[...] = jnp.zeros(out.shape, out.dtype)


def wait(order, *arrays):
    order.call(wait_kernel, "wait", [jax.ShapeDtypeStruct((8, 128), jnp.float32)], [], (), us=0.5, behind=arrays)


def last_kernel(keep, got, *refs):
    *done, out = refs
    rows = keep.shape[0]
    for k, x in enumerate(done):
        out[0, pl.ds(k * rows, rows), :] = x[...]
    out[0, pl.ds(len(done) * rows, rows), :] = (keep[...] + got[...].astype(jnp.float32)).astype(jnp.bfloat16)


def pack_kernel(*refs):
    *xs, out = refs
    rows = xs[0].shape[0]
    for k, x in enumerate(xs):
        out[0, pl.ds(k * rows, rows), :] = x[...]


def whole(order, kernel, name, args, rows):
    shape = jax.ShapeDtypeStruct((1, rows, args[0].shape[1]), jnp.bfloat16)
    return order.call(kernel, name, [shape], [VMEM_SPEC] * len(args), args, vmem=8 * MIB, us=0.5)[0]


def body(act, group_of, gain, w_in, w_out):
    place = lax.axis_index("section")
    g1 = group_of[0]
    prior = route(group_of, to_next_section)[0]
    g2 = jnp.where(place == 0, 1, prior).astype(jnp.int32)
    swap = (place % Y != Y - 1).astype(jnp.int32)
    idx1, idx2 = jnp.stack([g1, swap]), jnp.stack([g2, jnp.ones((), jnp.int32)])
    order = Order()

    def across(x):
        return route(x, to_x_neighbour)

    def onward(x):
        return route(x, to_next_section)

    def mirror(*xs):
        return route(whole(order, pack_kernel, "pack", xs, len(xs) * ROWS), to_mirror)

    rows = act.shape[1]
    r_in, r_out = route(w_in, to_other_core), route(w_out, to_other_core)
    own = [act[0, : rows // 2], act[0, rows // 2 :]]
    par = [across(x) for x in own]

    ((w_in1, w_out1, r_in1),) = pick(order, (g1,), (w_in, w_out, r_in))
    hidden = up_rows(order, idx1, own[0], par[0], gain, w_in1, r_in1)
    ((r_out1,),) = pick(order, (g1,), (r_out,))
    w1 = (w_in1, w_out1, r_in1, r_out1)
    give, keep0 = down(order, idx1, own[0], par[0], hidden, w_out1, r_out1, 0)
    got0 = across(give)
    give, keep1 = down(order, idx1, own[0], par[0], hidden, w_out1, r_out1, ROWS, (par[1], g2.reshape(1)))
    got1 = across(give)
    give, keep2 = block(order, idx1, own[1], par[1], gain, w1, 0, 0)
    got2 = across(give)
    x0 = onward(join(order, keep0, got0))
    give, keep3 = block(order, idx1, own[1], par[1], gain, w1, ROWS, ROWS)
    got3 = across(give)
    x1 = onward(join(order, keep1, got1))
    ((w_in2, w_out2),) = pick(order, (g2,), (w_in, w_out))
    x2 = onward(join(order, keep2, got2))
    ((r_in2, r_out2),) = pick(order, (g2,), (r_in, r_out), (x0,))
    x3 = onward(join(order, keep3, got3, (x1,)))
    w2 = (w_in2, w_out2, r_in2, r_out2)

    y0, y1, y2, y3 = (across(x) for x in (x0, x1, x2, x3))
    give, keep0 = block(order, idx2, x0, y0, gain, w2, us=1)
    got0 = across(give)
    low = mirror(x0, x1)
    give, keep1 = block(order, idx2, x1, y1, gain, w2, behind=(x2,), us=1)
    got1 = across(give)
    high = mirror(x2, x3)
    give, keep2 = block(order, idx2, x2, y2, gain, w2, us=1)
    got2 = across(give)
    give, keep3 = block(order, idx2, x3, y3, gain, w2, us=1)
    got3 = across(give)
    done = [join(order, keep0, got0, us=3)]
    wait(order, low)
    done.append(join(order, keep1, got1, us=3))
    wait(order, high)
    done.append(join(order, keep2, got2, us=3))
    stash = whole(order, pack_kernel, "pack", (low[0], high[0]), rows)
    return whole(order, last_kernel, "last", (keep3, got3, *done), rows), stash


def solution(mesh):
    placed = (
        P("section", "tensor", None),
        P("section"),
        P("section", None, None),
        P("section", None, None, "tensor"),
        P("section", None, "tensor", None),
    )
    return jax.shard_map(
        body,
        mesh=mesh,
        in_specs=placed,
        out_specs=(P("section", "tensor", None), P("section", "tensor", None)),
        check_vma=False,
    )
```

```python
import functools

import jax
import jax.numpy as jnp
from jax import lax
from jax.experimental import pallas as pl
from jax.experimental.pallas import tpu as pltpu
from jax.sharding import PartitionSpec as P

eps = 1e-05
AXES = ("section", "tensor")
Y = 4
HB = 512
MIB = 2**20
ROWS = 64


def route(x, to):
    sections, tensors = (lax.axis_size(a) for a in AXES)
    pairs = []
    for s in range(sections):
        for t in range(tensors):
            ds, dt = to(s, t, sections)
            pairs.append((s * tensors + t, ds * tensors + dt))
    return lax.ppermute(x, AXES, pairs)


def to_x_neighbour(s, t, n):
    return s, t ^ 2


def to_other_core(s, t, n):
    return s, t ^ 1


def to_next_section(s, t, n):
    return (s + 1) % n, (t ^ 2 if s % Y == Y - 1 else t)


def to_mirror(s, t, n):
    return n - 1 - s, t ^ 2


def in_vmem(x):
    return pltpu.with_memory_space_constraint(x, pltpu.VMEM)


def in_hbm(x):
    return pltpu.with_memory_space_constraint(x, pltpu.HBM)


class Order:
    def __init__(self):
        self.token = jnp.zeros((8, 128), jnp.float32)

    def call(self, kernel, name, outs, specs, args, scratch=(), vmem=4 * MIB, us=0.1, behind=(), out_specs=None, aliases=None):
        vmem_spec = pl.BlockSpec(memory_space=pltpu.VMEM)

        def with_token(*refs):
            ins = refs[: len(args)]
            rest = refs[len(args) + 1 + len(behind) :]
            rest[len(outs)][...] = jnp.zeros((8, 128), jnp.float32)
            kernel(*ins, *rest[: len(outs)], *rest[len(outs) + 1 :])

        *results, self.token = pl.pallas_call(
            with_token,
            out_shape=tuple(outs) + (jax.ShapeDtypeStruct((8, 128), jnp.float32),),
            in_specs=list(specs) + [pl.BlockSpec(memory_space=pl.ANY)] * (1 + len(behind)),
            out_specs=tuple(out_specs or (vmem_spec,) * len(outs)) + (vmem_spec,),
            input_output_aliases=aliases or {},
            scratch_shapes=list(scratch),
            compiler_params=pltpu.CompilerParams(vmem_limit_bytes=vmem),
            cost_estimate=pl.CostEstimate(flops=int(us * 1.15e9), bytes_accessed=2**14, transcendentals=0),
            name=name,
        )(*args, self.token, *behind)
        return results


SMEM_SPEC = pl.BlockSpec(memory_space=pltpu.SMEM)
VMEM_SPEC = pl.BlockSpec(memory_space=pltpu.VMEM)
HBM_SPEC = pl.BlockSpec(memory_space=pltpu.HBM)


def pick_kernel(groups, count, idx, *refs):
    ws, outs, sems = refs[:count], refs[count : (1 + groups) * count], refs[(1 + groups) * count]
    loads = []
    for j in range(groups):
        for n in range(count):
            for k in range(4):
                size = ws[n].shape[2] // 4
                piece = pl.ds(k * size, size)
                held = outs[j * count + n]
                loads.append(pltpu.make_async_copy(ws[n].at[0, idx[j], piece], held.at[piece], sems.at[len(loads)]))
    for load in loads:
        load.start()
    for load in loads:
        load.wait()


def pick(order, groups, ws, behind=()):
    n = len(ws)
    held = order.call(
        functools.partial(pick_kernel, len(groups), n),
        "pick_group",
        [pltpu.VMEM(w.shape[2:], w.dtype) for w in ws] * len(groups),
        [SMEM_SPEC] + [HBM_SPEC] * n,
        (jnp.stack(groups), *(in_hbm(w) for w in ws)),
        [pltpu.SemaphoreType.DMA((4 * n * len(groups),))],
        us=1.7 * n * len(groups),
        behind=behind,
    )
    return [held[j * n : (j + 1) * n] for j in range(len(groups))]


def normalize(x, gain_row):
    centred = x - jnp.mean(x, axis=-1, keepdims=True)
    spread = jnp.mean(centred * centred, axis=-1, keepdims=True)
    return (centred * lax.rsqrt(spread + eps) * gain_row).astype(jnp.bfloat16)


def up(normed, w):
    return jax.nn.gelu(jnp.dot(normed, w, preferred_element_type=jnp.float32), approximate=True).astype(jnp.bfloat16)


def prepare(idx, own, par, gain, normed):
    rows = own.shape[0]
    swapped = idx[1] == 1
    gain_row = jnp.where(idx[0] == 0, gain[0, 0:1, :], gain[0, 1:2, :]).astype(jnp.float32)
    x_own = own[...].astype(jnp.float32)
    x_par = par[...].astype(jnp.float32)
    normed[pl.ds(0, rows), :] = normalize(jnp.where(swapped, x_par, x_own), gain_row)
    normed[pl.ds(rows, rows), :] = normalize(jnp.where(swapped, x_own, x_par), gain_row)


def kept_rows(idx, own, par):
    return jnp.where(idx[1] == 1, par[...].astype(jnp.float32), own[...].astype(jnp.float32))


def window(ref, lo, rows):
    return ref.at[pl.ds(lo, rows)]


def block_kernel(own_lo, par_lo, idx, own, par, gain, w_in, w_out, r_in, r_out, give, keep, normed, total):
    rows = give.shape[0]
    own, par = window(own, own_lo, rows), window(par, par_lo, rows)
    prepare(idx, own, par, gain, normed)
    per = r_in.shape[1] // HB
    for b in range(2 * per):
        first, second = (w_in, w_out) if b < per else (r_in, r_out)
        piece = pl.ds((b % per) * HB, HB)
        part = jnp.dot(up(normed[...], first[:, piece]), second[piece, :], preferred_element_type=jnp.float32)
        if b == 0:
            total[...] = part
        elif b < 2 * per - 1:
            total[...] += part
        else:
            give[...] = (total[pl.ds(rows, rows), :] + part[rows:]).astype(jnp.bfloat16)
            keep[...] = kept_rows(idx, own, par) + (total[pl.ds(0, rows), :] + part[:rows])


def block(order, idx, own, par, gain, ws, own_lo=0, par_lo=0, behind=(), us=4):
    d = own.shape[1]
    return order.call(
        functools.partial(block_kernel, own_lo, par_lo),
        "block",
        [jax.ShapeDtypeStruct((ROWS, d), jnp.bfloat16), jax.ShapeDtypeStruct((ROWS, d), jnp.float32)],
        [SMEM_SPEC] + [VMEM_SPEC] * 7,
        (idx, own, par, gain, *(in_vmem(w) for w in ws)),
        [pltpu.VMEM((2 * ROWS, d), jnp.bfloat16), pltpu.VMEM((2 * ROWS, d), jnp.float32)],
        8 * MIB,
        us=us,
        behind=behind,
    )


def up_kernel(idx, own, par, gain, w_in, r_in, hidden, normed):
    for k in range(own.shape[0] // ROWS):
        prepare(idx, window(own, k * ROWS, ROWS), window(par, k * ROWS, ROWS), gain, window(normed, 2 * k * ROWS, 2 * ROWS))
    units = w_in.shape[1]
    for n, w in enumerate((w_in, r_in)):
        for lo in range(0, units, HB):
            hidden[:, pl.ds(n * units + lo, HB)] = up(normed[...], w[:, pl.ds(lo, HB)])


def up_rows(order, idx, own, par, gain, w_in, r_in):
    rows, d = own.shape
    return order.call(
        up_kernel,
        "up",
        [jax.ShapeDtypeStruct((2 * rows, 2 * w_in.shape[1]), jnp.bfloat16)],
        [SMEM_SPEC] + [VMEM_SPEC] * 5,
        (idx, own, par, gain, in_vmem(w_in), in_vmem(r_in)),
        [pltpu.VMEM((2 * rows, d), jnp.bfloat16)],
        8 * MIB,
        us=3,
    )[0]


def base_kernel(hidden, w_out, base):
    units = w_out.shape[0]
    base[...] = jnp.dot(hidden[:, pl.ds(0, units)], w_out[...], preferred_element_type=jnp.float32)


def base_rows(order, hidden, w_out):
    shape = jax.ShapeDtypeStruct((hidden.shape[0], w_out.shape[1]), jnp.float32)
    return order.call(base_kernel, "base", [shape], [VMEM_SPEC] * 2, (hidden, in_vmem(w_out)), vmem=8 * MIB, us=1.8)[0]


def finish(lo, idx, own, par, total, give, keep):
    rows = give.shape[0]
    give[...] = total[rows:].astype(jnp.bfloat16)
    keep[...] = kept_rows(idx, window(own, lo, rows), window(par, lo, rows)) + total[:rows]


def down_kernel(lo, idx, own, par, hidden, base, r_out, give, keep):
    units = r_out.shape[0]
    mine = pl.ds(2 * lo, 2 * give.shape[0])
    total = base[mine, :] + jnp.dot(hidden[mine, pl.ds(units, units)], r_out[...], preferred_element_type=jnp.float32)
    finish(lo, idx, own, par, total, give, keep)


def down_load_kernel(lo, idx, own, par, hidden, base, r_out, give, keep, held, sems):
    units, parts = held.shape[0], sems.shape[0]
    step = units // parts
    loads = []
    for k in range(parts):
        piece = pl.ds(k * step, step)
        loads.append(pltpu.make_async_copy(r_out.at[0, idx[0], piece], held.at[piece], sems.at[k]))
        loads[-1].start()
    mine = pl.ds(2 * lo, 2 * give.shape[0])
    total = base[mine, :]
    cut = parts // 2
    for half in range(2):
        for load in loads[half * cut : (half + 1) * cut]:
            load.wait()
        piece = pl.ds(half * cut * step, cut * step)
        total += jnp.dot(
            hidden[mine, pl.ds(units + half * cut * step, cut * step)], held[piece, :], preferred_element_type=jnp.float32
        )
    finish(lo, idx, own, par, total, give, keep)


def down(order, idx, own, par, hidden, base, r_out, lo, behind=()):
    d = own.shape[1]
    loading = r_out.ndim > 2
    return order.call(
        functools.partial(down_load_kernel if loading else down_kernel, lo),
        "down",
        [jax.ShapeDtypeStruct((ROWS, d), jnp.bfloat16), jax.ShapeDtypeStruct((ROWS, d), jnp.float32)]
        + [pltpu.VMEM(r_out.shape[2:], r_out.dtype)] * loading,
        [SMEM_SPEC] + [VMEM_SPEC] * 4 + [HBM_SPEC if loading else VMEM_SPEC],
        (idx, own, par, hidden, base, in_hbm(r_out) if loading else in_vmem(r_out)),
        [pltpu.SemaphoreType.DMA((8,))] * loading,
        vmem=8 * MIB,
        us=2,
        behind=behind,
    )


def join_kernel(keep, got, out):
    out[...] = (keep[...] + got[...].astype(jnp.float32)).astype(jnp.bfloat16)


def join(order, keep, got, behind=(), us=0.5):
    shape = jax.ShapeDtypeStruct(got.shape, jnp.bfloat16)
    return order.call(join_kernel, "join", [shape], [VMEM_SPEC] * 2, (keep, got), us=us, behind=behind)[0]


def wait_kernel(out):
    out[...] = jnp.zeros(out.shape, out.dtype)


def wait(order, *arrays):
    order.call(wait_kernel, "wait", [jax.ShapeDtypeStruct((8, 128), jnp.float32)], [], (), us=0.5, behind=arrays)


def last_kernel(keep, got, *refs):
    *done, out = refs
    rows = keep.shape[0]
    for k, x in enumerate(done):
        out[0, pl.ds(k * rows, rows), :] = x[...]
    out[0, pl.ds(len(done) * rows, rows), :] = (keep[...] + got[...].astype(jnp.float32)).astype(jnp.bfloat16)


def pack_kernel(*refs):
    *xs, out = refs
    rows = xs[0].shape[0]
    for k, x in enumerate(xs):
        out[0, pl.ds(k * rows, rows), :] = x[...]


def whole(order, kernel, name, args, rows):
    shape = jax.ShapeDtypeStruct((1, rows, args[0].shape[1]), jnp.bfloat16)
    return order.call(kernel, name, [shape], [VMEM_SPEC] * len(args), args, vmem=8 * MIB, us=0.5)[0]


def body(act, group_of, gain, w_in, w_out):
    place = lax.axis_index("section")
    g1 = group_of[0]
    prior = route(group_of, to_next_section)[0]
    g2 = jnp.where(place == 0, 1, prior).astype(jnp.int32)
    swap = (place % Y != Y - 1).astype(jnp.int32)
    idx1, idx2 = jnp.stack([g1, swap]), jnp.stack([g2, jnp.ones((), jnp.int32)])
    order = Order()

    def across(x):
        return route(x, to_x_neighbour)

    def onward(x):
        return route(x, to_next_section)

    def mirror(*xs):
        return route(whole(order, pack_kernel, "pack", xs, len(xs) * ROWS), to_mirror)

    rows = act.shape[1]
    r_in, r_out = route(w_in, to_other_core), route(w_out, to_other_core)
    own = [act[0, : rows // 2], act[0, rows // 2 :]]
    par = [across(x) for x in own]

    ((w_in1, w_out1, r_in1),) = pick(order, (g1,), (w_in, w_out, r_in))
    hidden = up_rows(order, idx1, own[0], par[0], gain, w_in1, r_in1)
    base = base_rows(order, hidden, w_out1)
    give, keep0, r_out1 = down(order, idx1, own[0], par[0], hidden, base, r_out, 0)
    w1 = (w_in1, w_out1, r_in1, r_out1)
    got0 = across(give)
    give, keep1 = down(order, idx1, own[0], par[0], hidden, base, r_out1, ROWS, (par[1], g2.reshape(1)))
    got1 = across(give)
    give, keep2 = block(order, idx1, own[1], par[1], gain, w1, 0, 0)
    got2 = across(give)
    x0 = onward(join(order, keep0, got0))
    give, keep3 = block(order, idx1, own[1], par[1], gain, w1, ROWS, ROWS)
    got3 = across(give)
    x1 = onward(join(order, keep1, got1))
    ((w_in2, w_out2),) = pick(order, (g2,), (w_in, w_out))
    x2 = onward(join(order, keep2, got2))
    ((r_in2, r_out2),) = pick(order, (g2,), (r_in, r_out), (x0,))
    x3 = onward(join(order, keep3, got3, (x1,)))
    w2 = (w_in2, w_out2, r_in2, r_out2)

    y0, y1, y2, y3 = (across(x) for x in (x0, x1, x2, x3))
    give, keep0 = block(order, idx2, x0, y0, gain, w2, us=1)
    got0 = across(give)
    low = mirror(x0, x1)
    give, keep1 = block(order, idx2, x1, y1, gain, w2, behind=(x2,), us=1)
    got1 = across(give)
    high = mirror(x2, x3)
    give, keep2 = block(order, idx2, x2, y2, gain, w2, us=1)
    got2 = across(give)
    give, keep3 = block(order, idx2, x3, y3, gain, w2, us=1)
    got3 = across(give)
    done = [join(order, keep0, got0, us=3)]
    wait(order, low)
    done.append(join(order, keep1, got1, us=3))
    wait(order, high)
    done.append(join(order, keep2, got2, us=3))
    stash = whole(order, pack_kernel, "pack", (low[0], high[0]), rows)
    return whole(order, last_kernel, "last", (keep3, got3, *done), rows), stash


def solution(mesh):
    placed = (
        P("section", "tensor", None),
        P("section"),
        P("section", None, None),
        P("section", None, None, "tensor"),
        P("section", None, "tensor", None),
    )
    return jax.shard_map(
        body,
        mesh=mesh,
        in_specs=placed,
        out_specs=(P("section", "tensor", None), P("section", "tensor", None)),
        check_vma=False,
    )
```

```python
import functools

import jax
import jax.numpy as jnp
from jax import lax
from jax.experimental import pallas as pl
from jax.experimental.pallas import tpu as pltpu
from jax.sharding import PartitionSpec as P

eps = 1e-05
AXES = ("section", "tensor")
Y = 4
HB = 512
MIB = 2**20
ROWS = 64


def route(x, to):
    sections, tensors = (lax.axis_size(a) for a in AXES)
    pairs = []
    for s in range(sections):
        for t in range(tensors):
            ds, dt = to(s, t, sections)
            pairs.append((s * tensors + t, ds * tensors + dt))
    return lax.ppermute(x, AXES, pairs)


def to_x_neighbour(s, t, n):
    return s, t ^ 2


def to_other_core(s, t, n):
    return s, t ^ 1


def to_next_section(s, t, n):
    return (s + 1) % n, (t ^ 2 if s % Y == Y - 1 else t)


def to_mirror(s, t, n):
    return n - 1 - s, t ^ 2


def in_vmem(x):
    return pltpu.with_memory_space_constraint(x, pltpu.VMEM)


def in_hbm(x):
    return pltpu.with_memory_space_constraint(x, pltpu.HBM)


class Order:
    def __init__(self):
        self.token = jnp.zeros((8, 128), jnp.float32)

    def call(self, kernel, name, outs, specs, args, scratch=(), vmem=4 * MIB, us=0.1, behind=(), out_specs=None):
        vmem_spec = pl.BlockSpec(memory_space=pltpu.VMEM)

        def with_token(*refs):
            ins = refs[: len(args)]
            rest = refs[len(args) + 1 + len(behind) :]
            rest[len(outs)][...] = jnp.zeros((8, 128), jnp.float32)
            kernel(*ins, *rest[: len(outs)], *rest[len(outs) + 1 :])

        *results, self.token = pl.pallas_call(
            with_token,
            out_shape=tuple(outs) + (jax.ShapeDtypeStruct((8, 128), jnp.float32),),
            in_specs=list(specs) + [pl.BlockSpec(memory_space=pl.ANY)] * (1 + len(behind)),
            out_specs=tuple(out_specs or (vmem_spec,) * len(outs)) + (vmem_spec,),
            scratch_shapes=list(scratch),
            compiler_params=pltpu.CompilerParams(vmem_limit_bytes=vmem),
            cost_estimate=pl.CostEstimate(flops=int(us * 1.15e9), bytes_accessed=2**14, transcendentals=0),
            name=name,
        )(*args, self.token, *behind)
        return results


SMEM_SPEC = pl.BlockSpec(memory_space=pltpu.SMEM)
VMEM_SPEC = pl.BlockSpec(memory_space=pltpu.VMEM)
HBM_SPEC = pl.BlockSpec(memory_space=pltpu.HBM)


def pick_kernel(groups, count, idx, *refs):
    ws, outs, sems = refs[:count], refs[count : (1 + groups) * count], refs[(1 + groups) * count]
    loads = []
    for j in range(groups):
        for n in range(count):
            for k in range(4):
                size = ws[n].shape[2] // 4
                piece = pl.ds(k * size, size)
                held = outs[j * count + n]
                loads.append(pltpu.make_async_copy(ws[n].at[0, idx[j * count + n], piece], held.at[piece], sems.at[len(loads)]))
    for load in loads:
        load.start()
    for load in loads:
        load.wait()


def pick(order, groups, ws, behind=(), us=None):
    n = len(ws)
    held = order.call(
        functools.partial(pick_kernel, len(groups), n),
        "pick_group",
        [pltpu.VMEM(w.shape[2:], w.dtype) for w in ws] * len(groups),
        [SMEM_SPEC] + [HBM_SPEC] * n,
        (jnp.stack([g[i] if isinstance(g, tuple) else g for g in groups for i in range(n)]), *(in_hbm(w) for w in ws)),
        [pltpu.SemaphoreType.DMA((4 * n * len(groups),))],
        us=us or 1.7 * n * len(groups),
        behind=behind,
    )
    return [held[j * n : (j + 1) * n] for j in range(len(groups))]


def copy_kernel(idx, w, sent, held, in_sems, out_sems):
    parts = in_sems.shape[0]
    pieces = [pl.ds(k * (held.shape[0] // parts), held.shape[0] // parts) for k in range(parts)]
    loads = [pltpu.make_async_copy(w.at[0, idx[0], p], held.at[p], in_sems.at[k]) for k, p in enumerate(pieces)]
    saves = [pltpu.make_async_copy(held.at[p], sent.at[0, 0, p], out_sems.at[k]) for k, p in enumerate(pieces)]
    for load in loads:
        load.start()
    for load, save in zip(loads, saves):
        load.wait()
        save.start()
    for save in saves:
        save.wait()


def copy_group(order, group, w, us):
    shape = w.shape[2:]
    return order.call(
        copy_kernel,
        "copy_group",
        [pltpu.HBM((1, 1) + shape, w.dtype)],
        [SMEM_SPEC, HBM_SPEC],
        (group.reshape(1), in_hbm(w)),
        [pltpu.VMEM(shape, w.dtype), pltpu.SemaphoreType.DMA((8,)), pltpu.SemaphoreType.DMA((8,))],
        vmem=6 * MIB,
        us=us,
        out_specs=[HBM_SPEC],
    )[0]


def load_kernel(idx, first, second, held, sems):
    parts = sems.shape[0]
    pieces = [pl.ds(k * (held.shape[0] // parts), held.shape[0] // parts) for k in range(parts)]

    def run(w):
        loads = [pltpu.make_async_copy(w.at[0, 0, p], held.at[p], sems.at[k]) for k, p in enumerate(pieces)]
        for load in loads:
            load.start()
        for load in loads:
            load.wait()

    pl.when(idx[0] == 0)(lambda: run(first))
    pl.when(idx[0] != 0)(lambda: run(second))


def load(order, which, first, second):
    return order.call(
        load_kernel,
        "load",
        [pltpu.VMEM(first.shape[2:], first.dtype)],
        [SMEM_SPEC, HBM_SPEC, HBM_SPEC],
        (which.reshape(1), in_hbm(first), in_hbm(second)),
        [pltpu.SemaphoreType.DMA((8,))],
        us=1.7,
    )[0]


def normalize(x, gain_row):
    centred = x - jnp.mean(x, axis=-1, keepdims=True)
    spread = jnp.mean(centred * centred, axis=-1, keepdims=True)
    return (centred * lax.rsqrt(spread + eps) * gain_row).astype(jnp.bfloat16)


def up(normed, w):
    return jax.nn.gelu(jnp.dot(normed, w, preferred_element_type=jnp.float32), approximate=True).astype(jnp.bfloat16)


def prepare(idx, own, par, gain, normed):
    rows = own.shape[0]
    swapped = idx[1] == 1
    gain_row = jnp.where(idx[0] == 0, gain[0, 0:1, :], gain[0, 1:2, :]).astype(jnp.float32)
    x_own = own[...].astype(jnp.float32)
    x_par = par[...].astype(jnp.float32)
    normed[pl.ds(0, rows), :] = normalize(jnp.where(swapped, x_par, x_own), gain_row)
    normed[pl.ds(rows, rows), :] = normalize(jnp.where(swapped, x_own, x_par), gain_row)


def kept_rows(idx, own, par):
    return jnp.where(idx[1] == 1, par[...].astype(jnp.float32), own[...].astype(jnp.float32))


def window(ref, lo, rows):
    return ref.at[pl.ds(lo, rows)]


def block_kernel(own_lo, par_lo, idx, own, par, gain, w_in, w_out, r_in, r_out, give, keep, normed, total):
    rows = give.shape[0]
    own, par = window(own, own_lo, rows), window(par, par_lo, rows)
    prepare(idx, own, par, gain, normed)
    per = r_in.shape[1] // HB
    for b in range(2 * per):
        first, second = (w_in, w_out) if b < per else (r_in, r_out)
        piece = pl.ds((b % per) * HB, HB)
        part = jnp.dot(up(normed[...], first[:, piece]), second[piece, :], preferred_element_type=jnp.float32)
        if b == 0:
            total[...] = part
        elif b < 2 * per - 1:
            total[...] += part
        else:
            give[...] = (total[pl.ds(rows, rows), :] + part[rows:]).astype(jnp.bfloat16)
            keep[...] = kept_rows(idx, own, par) + (total[pl.ds(0, rows), :] + part[:rows])


def block(order, idx, own, par, gain, ws, own_lo=0, par_lo=0, behind=(), us=4):
    d = own.shape[1]
    return order.call(
        functools.partial(block_kernel, own_lo, par_lo),
        "block",
        [jax.ShapeDtypeStruct((ROWS, d), jnp.bfloat16), jax.ShapeDtypeStruct((ROWS, d), jnp.float32)],
        [SMEM_SPEC] + [VMEM_SPEC] * 7,
        (idx, own, par, gain, *(in_vmem(w) for w in ws)),
        [pltpu.VMEM((2 * ROWS, d), jnp.bfloat16), pltpu.VMEM((2 * ROWS, d), jnp.float32)],
        8 * MIB,
        us=us,
        behind=behind,
    )


def up_kernel(idx, own, par, gain, w_in, r_in, hidden, normed):
    for k in range(own.shape[0] // ROWS):
        prepare(idx, window(own, k * ROWS, ROWS), window(par, k * ROWS, ROWS), gain, window(normed, 2 * k * ROWS, 2 * ROWS))
    units = w_in.shape[1]
    for n, w in enumerate((w_in, r_in)):
        for lo in range(0, units, HB):
            hidden[:, pl.ds(n * units + lo, HB)] = up(normed[...], w[:, pl.ds(lo, HB)])


def up_rows(order, idx, own, par, gain, w_in, r_in):
    rows, d = own.shape
    return order.call(
        up_kernel,
        "up",
        [jax.ShapeDtypeStruct((2 * rows, 2 * w_in.shape[1]), jnp.bfloat16)],
        [SMEM_SPEC] + [VMEM_SPEC] * 5,
        (idx, own, par, gain, in_vmem(w_in), in_vmem(r_in)),
        [pltpu.VMEM((2 * rows, d), jnp.bfloat16)],
        8 * MIB,
        us=50,
    )[0]


def down_kernel(lo, idx, own, par, hidden, w_out, r_out, give, keep):
    rows = give.shape[0]
    units = w_out.shape[0]
    mine = window(hidden, 2 * lo, 2 * rows)
    total = jnp.dot(mine[:, pl.ds(0, units)], w_out[...], preferred_element_type=jnp.float32)
    total += jnp.dot(mine[:, pl.ds(units, units)], r_out[...], preferred_element_type=jnp.float32)
    give[...] = total[rows:].astype(jnp.bfloat16)
    keep[...] = kept_rows(idx, window(own, lo, rows), window(par, lo, rows)) + total[:rows]


def down(order, idx, own, par, hidden, w_out, r_out, lo, behind=()):
    d = own.shape[1]
    return order.call(
        functools.partial(down_kernel, lo),
        "down",
        [jax.ShapeDtypeStruct((ROWS, d), jnp.bfloat16), jax.ShapeDtypeStruct((ROWS, d), jnp.float32)],
        [SMEM_SPEC] + [VMEM_SPEC] * 5,
        (idx, own, par, hidden, in_vmem(w_out), in_vmem(r_out)),
        vmem=8 * MIB,
        us=2,
        behind=behind,
    )


def join_kernel(keep, got, out):
    out[...] = (keep[...] + got[...].astype(jnp.float32)).astype(jnp.bfloat16)


def join(order, keep, got, behind=(), us=0.5):
    shape = jax.ShapeDtypeStruct(got.shape, jnp.bfloat16)
    return order.call(join_kernel, "join", [shape], [VMEM_SPEC] * 2, (keep, got), us=us, behind=behind)[0]


def wait_kernel(out):
    out[...] = jnp.zeros(out.shape, out.dtype)


def wait(order, *arrays):
    order.call(wait_kernel, "wait", [jax.ShapeDtypeStruct((8, 128), jnp.float32)], [], (), us=0.5, behind=arrays)


def last_kernel(keep, got, *refs):
    *done, out = refs
    rows = keep.shape[0]
    for k, x in enumerate(done):
        out[0, pl.ds(k * rows, rows), :] = x[...]
    out[0, pl.ds(len(done) * rows, rows), :] = (keep[...] + got[...].astype(jnp.float32)).astype(jnp.bfloat16)


def pack_kernel(*refs):
    *xs, out = refs
    rows = xs[0].shape[0]
    for k, x in enumerate(xs):
        out[0, pl.ds(k * rows, rows), :] = x[...]


def whole(order, kernel, name, args, rows):
    shape = jax.ShapeDtypeStruct((1, rows, args[0].shape[1]), jnp.bfloat16)
    return order.call(kernel, name, [shape], [VMEM_SPEC] * len(args), args, vmem=8 * MIB, us=0.5)[0]


def body(act, group_of, gain, w_in, w_out):
    place = lax.axis_index("section")
    g1 = group_of[0]
    prior = route(group_of, to_next_section)[0]
    g2 = jnp.where(place == 0, 1, prior).astype(jnp.int32)
    swap = (place % Y != Y - 1).astype(jnp.int32)
    idx1, idx2 = jnp.stack([g1, swap]), jnp.stack([g2, jnp.ones((), jnp.int32)])
    order = Order()

    def across(x):
        return route(x, to_x_neighbour)

    def onward(x):
        return route(x, to_next_section)

    def mirror(*xs):
        return route(whole(order, pack_kernel, "pack", xs, len(xs) * ROWS), to_mirror)

    rows = act.shape[1]
    r_in = route(w_in, to_other_core)
    own = [act[0, : rows // 2], act[0, rows // 2 :]]
    par = [across(x) for x in own]

    r_first = route(copy_group(order, g1, w_out, 0.05), to_other_core)
    r_second = route(copy_group(order, 1 - g1, w_out, 0.05), to_other_core)
    ((w_in1, w_out1, r_in1),) = pick(order, (g1,), (w_in, w_out, r_in), us=0.1)
    hidden = up_rows(order, idx1, own[0], par[0], gain, w_in1, r_in1)
    ((r_out1,),) = pick(order, (jnp.zeros_like(g1),), (r_first,))
    w1 = (w_in1, w_out1, r_in1, r_out1)
    give, keep0 = down(order, idx1, own[0], par[0], hidden, w_out1, r_out1, 0)
    got0 = across(give)
    give, keep1 = down(order, idx1, own[0], par[0], hidden, w_out1, r_out1, ROWS, (par[1], g2.reshape(1)))
    got1 = across(give)
    give, keep2 = block(order, idx1, own[1], par[1], gain, w1, 0, 0)
    got2 = across(give)
    x0 = onward(join(order, keep0, got0))
    give, keep3 = block(order, idx1, own[1], par[1], gain, w1, ROWS, ROWS)
    got3 = across(give)
    x1 = onward(join(order, keep1, got1))
    ((w_in2, w_out2),) = pick(order, (g2,), (w_in, w_out))
    x2 = onward(join(order, keep2, got2))
    ((r_in2,),) = pick(order, (g2,), (r_in,), (x0,))
    r_out2 = load(order, g2 - g1, r_first, r_second)
    x3 = onward(join(order, keep3, got3, (x1,)))
    w2 = (w_in2, w_out2, r_in2, r_out2)

    y0, y1, y2, y3 = (across(x) for x in (x0, x1, x2, x3))
    give, keep0 = block(order, idx2, x0, y0, gain, w2, us=1)
    got0 = across(give)
    low = mirror(x0, x1)
    give, keep1 = block(order, idx2, x1, y1, gain, w2, behind=(x2,), us=1)
    got1 = across(give)
    high = mirror(x2, x3)
    give, keep2 = block(order, idx2, x2, y2, gain, w2, us=1)
    got2 = across(give)
    give, keep3 = block(order, idx2, x3, y3, gain, w2, us=1)
    got3 = across(give)
    done = [join(order, keep0, got0, us=3)]
    wait(order, low)
    done.append(join(order, keep1, got1, us=3))
    wait(order, high)
    done.append(join(order, keep2, got2, us=3))
    stash = whole(order, pack_kernel, "pack", (low[0], high[0]), rows)
    return whole(order, last_kernel, "last", (keep3, got3, *done), rows), stash


def solution(mesh):
    placed = (
        P("section", "tensor", None),
        P("section"),
        P("section", None, None),
        P("section", None, None, "tensor"),
        P("section", None, "tensor", None),
    )
    return jax.shard_map(
        body,
        mesh=mesh,
        in_specs=placed,
        out_specs=(P("section", "tensor", None), P("section", "tensor", None)),
        check_vma=False,
    )
```

```python
import functools

import jax
import jax.numpy as jnp
from jax import lax
from jax.experimental import pallas as pl
from jax.experimental.pallas import tpu as pltpu
from jax.sharding import PartitionSpec as P

eps = 1e-05
AXES = ("section", "tensor")
Y = 4
HB = 1024
MIB = 2**20
ROWS = 64


def route(x, to):
    sections, tensors = (lax.axis_size(a) for a in AXES)
    pairs = []
    for s in range(sections):
        for t in range(tensors):
            ds, dt = to(s, t, sections)
            pairs.append((s * tensors + t, ds * tensors + dt))
    return lax.ppermute(x, AXES, pairs)


def to_x_neighbour(s, t, n):
    return s, t ^ 2


def to_other_core(s, t, n):
    return s, t ^ 1


def to_next_section(s, t, n):
    return (s + 1) % n, (t ^ 2 if s % Y == Y - 1 else t)


def to_mirror(s, t, n):
    return n - 1 - s, t ^ 2


def in_vmem(x):
    return pltpu.with_memory_space_constraint(x, pltpu.VMEM)


def in_hbm(x):
    return pltpu.with_memory_space_constraint(x, pltpu.HBM)


class Order:
    def __init__(self):
        self.token = jnp.zeros((8, 128), jnp.float32)

    def call(self, kernel, name, outs, specs, args, scratch=(), vmem=4 * MIB, us=0.1, behind=(), out_specs=None):
        vmem_spec = pl.BlockSpec(memory_space=pltpu.VMEM)

        def with_token(*refs):
            ins = refs[: len(args)]
            rest = refs[len(args) + 1 + len(behind) :]
            rest[len(outs)][...] = jnp.zeros((8, 128), jnp.float32)
            kernel(*ins, *rest[: len(outs)], *rest[len(outs) + 1 :])

        *results, self.token = pl.pallas_call(
            with_token,
            out_shape=tuple(outs) + (jax.ShapeDtypeStruct((8, 128), jnp.float32),),
            in_specs=list(specs) + [pl.BlockSpec(memory_space=pl.ANY)] * (1 + len(behind)),
            out_specs=tuple(out_specs or (vmem_spec,) * len(outs)) + (vmem_spec,),
            scratch_shapes=list(scratch),
            compiler_params=pltpu.CompilerParams(vmem_limit_bytes=vmem),
            cost_estimate=pl.CostEstimate(flops=int(us * 1.15e9), bytes_accessed=2**14, transcendentals=0),
            name=name,
        )(*args, self.token, *behind)
        return results


SMEM_SPEC = pl.BlockSpec(memory_space=pltpu.SMEM)
VMEM_SPEC = pl.BlockSpec(memory_space=pltpu.VMEM)
HBM_SPEC = pl.BlockSpec(memory_space=pltpu.HBM)


def pick_kernel(groups, count, idx, *refs):
    ws, outs, sems = refs[:count], refs[count : (1 + groups) * count], refs[(1 + groups) * count]
    loads = []
    for j in range(groups):
        for n in range(count):
            for k in range(4):
                size = ws[n].shape[2] // 4
                piece = pl.ds(k * size, size)
                held = outs[j * count + n]
                loads.append(pltpu.make_async_copy(ws[n].at[0, idx[j * count + n], piece], held.at[piece], sems.at[len(loads)]))
    for load in loads:
        load.start()
    for load in loads:
        load.wait()


def pick(order, groups, ws, behind=(), us=None):
    n = len(ws)
    held = order.call(
        functools.partial(pick_kernel, len(groups), n),
        "pick_group",
        [pltpu.VMEM(w.shape[2:], w.dtype) for w in ws] * len(groups),
        [SMEM_SPEC] + [HBM_SPEC] * n,
        (jnp.stack([g[i] if isinstance(g, tuple) else g for g in groups for i in range(n)]), *(in_hbm(w) for w in ws)),
        [pltpu.SemaphoreType.DMA((4 * n * len(groups),))],
        us=us or 1.7 * n * len(groups),
        behind=behind,
    )
    return [held[j * n : (j + 1) * n] for j in range(len(groups))]


def copy_kernel(idx, w, sent, held, in_sems, out_sems):
    parts = in_sems.shape[0]
    pieces = [pl.ds(k * (held.shape[0] // parts), held.shape[0] // parts) for k in range(parts)]
    loads = [pltpu.make_async_copy(w.at[0, idx[0], p], held.at[p], in_sems.at[k]) for k, p in enumerate(pieces)]
    saves = [pltpu.make_async_copy(held.at[p], sent.at[0, 0, p], out_sems.at[k]) for k, p in enumerate(pieces)]
    for load in loads:
        load.start()
    for load, save in zip(loads, saves):
        load.wait()
        save.start()
    for save in saves:
        save.wait()


def copy_group(order, group, w, us):
    shape = w.shape[2:]
    return order.call(
        copy_kernel,
        "copy_group",
        [pltpu.HBM((1, 1) + shape, w.dtype)],
        [SMEM_SPEC, HBM_SPEC],
        (group.reshape(1), in_hbm(w)),
        [pltpu.VMEM(shape, w.dtype), pltpu.SemaphoreType.DMA((8,)), pltpu.SemaphoreType.DMA((8,))],
        vmem=6 * MIB,
        us=us,
        out_specs=[HBM_SPEC],
    )[0]


def load_kernel(idx, w, first, second, held_w, held, sems):
    parts = sems.shape[0] // 2

    def pieces(ref):
        size = ref.shape[0] // parts
        return [pl.ds(k * size, size) for k in range(parts)]

    loads = [pltpu.make_async_copy(w.at[0, idx[0], p], held_w.at[p], sems.at[k]) for k, p in enumerate(pieces(held_w))]
    for load in loads:
        load.start()

    def run(ref):
        more = [pltpu.make_async_copy(ref.at[0, 0, p], held.at[p], sems.at[parts + k]) for k, p in enumerate(pieces(held))]
        for load in more:
            load.start()
        for load in more:
            load.wait()

    pl.when(idx[1] == 0)(lambda: run(first))
    pl.when(idx[1] != 0)(lambda: run(second))
    for load in loads:
        load.wait()


def load(order, group, which, w, first, second, behind=()):
    return order.call(
        load_kernel,
        "load",
        [pltpu.VMEM(w.shape[2:], w.dtype), pltpu.VMEM(first.shape[2:], first.dtype)],
        [SMEM_SPEC, HBM_SPEC, HBM_SPEC, HBM_SPEC],
        (jnp.stack([group, which]), in_hbm(w), in_hbm(first), in_hbm(second)),
        [pltpu.SemaphoreType.DMA((8,))],
        us=3.4,
        behind=behind,
    )


def normalize(x, gain_row):
    centred = x - jnp.mean(x, axis=-1, keepdims=True)
    spread = jnp.mean(centred * centred, axis=-1, keepdims=True)
    return (centred * lax.rsqrt(spread + eps) * gain_row).astype(jnp.bfloat16)


def up(normed, w):
    return jax.nn.gelu(jnp.dot(normed, w, preferred_element_type=jnp.float32), approximate=True).astype(jnp.bfloat16)


def prepare(idx, own, par, gain, normed):
    rows = own.shape[0]
    swapped = idx[1] == 1
    gain_row = jnp.where(idx[0] == 0, gain[0, 0:1, :], gain[0, 1:2, :]).astype(jnp.float32)
    x_own = own[...].astype(jnp.float32)
    x_par = par[...].astype(jnp.float32)
    normed[pl.ds(0, rows), :] = normalize(jnp.where(swapped, x_par, x_own), gain_row)
    normed[pl.ds(rows, rows), :] = normalize(jnp.where(swapped, x_own, x_par), gain_row)


def kept_rows(idx, own, par):
    return jnp.where(idx[1] == 1, par[...].astype(jnp.float32), own[...].astype(jnp.float32))


def window(ref, lo, rows):
    return ref.at[pl.ds(lo, rows)]


def block_kernel(own_lo, par_lo, idx, own, par, gain, w_in, w_out, r_in, r_out, give, keep, normed, total):
    rows = give.shape[0]
    own, par = window(own, own_lo, rows), window(par, par_lo, rows)
    prepare(idx, own, par, gain, normed)
    per = r_in.shape[1] // HB
    for b in range(2 * per):
        first, second = (w_in, w_out) if b < per else (r_in, r_out)
        piece = pl.ds((b % per) * HB, HB)
        part = jnp.dot(up(normed[...], first[:, piece]), second[piece, :], preferred_element_type=jnp.float32)
        if b == 0:
            total[...] = part
        elif b < 2 * per - 1:
            total[...] += part
        else:
            give[...] = (total[pl.ds(rows, rows), :] + part[rows:]).astype(jnp.bfloat16)
            keep[...] = kept_rows(idx, own, par) + (total[pl.ds(0, rows), :] + part[:rows])


def block(order, idx, own, par, gain, ws, own_lo=0, par_lo=0, behind=(), us=4):
    d = own.shape[1]
    return order.call(
        functools.partial(block_kernel, own_lo, par_lo),
        "block",
        [jax.ShapeDtypeStruct((ROWS, d), jnp.bfloat16), jax.ShapeDtypeStruct((ROWS, d), jnp.float32)],
        [SMEM_SPEC] + [VMEM_SPEC] * 7,
        (idx, own, par, gain, *(in_vmem(w) for w in ws)),
        [pltpu.VMEM((2 * ROWS, d), jnp.bfloat16), pltpu.VMEM((2 * ROWS, d), jnp.float32)],
        8 * MIB,
        us=us,
        behind=behind,
    )


def up_kernel(idx, own, par, gain, w_in, r_in, hidden, normed):
    for k in range(own.shape[0] // ROWS):
        prepare(idx, window(own, k * ROWS, ROWS), window(par, k * ROWS, ROWS), gain, window(normed, 2 * k * ROWS, 2 * ROWS))
    units = w_in.shape[1]
    for n, w in enumerate((w_in, r_in)):
        for lo in range(0, units, HB):
            hidden[:, pl.ds(n * units + lo, HB)] = up(normed[...], w[:, pl.ds(lo, HB)])


def up_rows(order, idx, own, par, gain, w_in, r_in):
    rows, d = own.shape
    return order.call(
        up_kernel,
        "up",
        [jax.ShapeDtypeStruct((2 * rows, 2 * w_in.shape[1]), jnp.bfloat16)],
        [SMEM_SPEC] + [VMEM_SPEC] * 5,
        (idx, own, par, gain, in_vmem(w_in), in_vmem(r_in)),
        [pltpu.VMEM((2 * rows, d), jnp.bfloat16)],
        8 * MIB,
        us=50,
    )[0]


def down_kernel(lo, idx, own, par, hidden, w_out, r_out, give, keep):
    rows = give.shape[0]
    units = w_out.shape[0]
    mine = window(hidden, 2 * lo, 2 * rows)
    total = jnp.dot(mine[:, pl.ds(0, units)], w_out[...], preferred_element_type=jnp.float32)
    total += jnp.dot(mine[:, pl.ds(units, units)], r_out[...], preferred_element_type=jnp.float32)
    give[...] = total[rows:].astype(jnp.bfloat16)
    keep[...] = kept_rows(idx, window(own, lo, rows), window(par, lo, rows)) + total[:rows]


def down_load_kernel(lo, idx, own, par, hidden, w_out, r_out, give, keep, held, sems):
    rows = give.shape[0]
    units, parts = w_out.shape[0], sems.shape[0]
    step = units // parts
    loads = []
    for k in range(parts):
        piece = pl.ds(k * step, step)
        loads.append(pltpu.make_async_copy(r_out.at[0, 0, piece], held.at[piece], sems.at[k]))
        loads[-1].start()
    mine = pl.ds(2 * lo, 2 * rows)
    total = jnp.dot(hidden[mine, pl.ds(0, units)], w_out[...], preferred_element_type=jnp.float32)
    cut = parts // 2
    for half in range(2):
        for load in loads[half * cut : (half + 1) * cut]:
            load.wait()
        first, size = half * cut * step, cut * step
        total += jnp.dot(
            hidden[mine, pl.ds(units + first, size)], held[pl.ds(first, size), :], preferred_element_type=jnp.float32
        )
    give[...] = total[rows:].astype(jnp.bfloat16)
    keep[...] = kept_rows(idx, window(own, lo, rows), window(par, lo, rows)) + total[:rows]


def down_load(order, idx, own, par, hidden, w_out, r_out, lo):
    d = own.shape[1]
    return order.call(
        functools.partial(down_load_kernel, lo),
        "down_load",
        [jax.ShapeDtypeStruct((ROWS, d), jnp.bfloat16), jax.ShapeDtypeStruct((ROWS, d), jnp.float32)]
        + [pltpu.VMEM(r_out.shape[2:], r_out.dtype)],
        [SMEM_SPEC] + [VMEM_SPEC] * 4 + [HBM_SPEC],
        (idx, own, par, hidden, in_vmem(w_out), in_hbm(r_out)),
        [pltpu.SemaphoreType.DMA((8,))],
        vmem=8 * MIB,
        us=2,
    )


def down(order, idx, own, par, hidden, w_out, r_out, lo, behind=()):
    d = own.shape[1]
    return order.call(
        functools.partial(down_kernel, lo),
        "down",
        [jax.ShapeDtypeStruct((ROWS, d), jnp.bfloat16), jax.ShapeDtypeStruct((ROWS, d), jnp.float32)],
        [SMEM_SPEC] + [VMEM_SPEC] * 5,
        (idx, own, par, hidden, in_vmem(w_out), in_vmem(r_out)),
        vmem=8 * MIB,
        us=2,
        behind=behind,
    )


def join_kernel(keep, got, out):
    out[...] = (keep[...] + got[...].astype(jnp.float32)).astype(jnp.bfloat16)


def join(order, keep, got, behind=(), us=0.5):
    shape = jax.ShapeDtypeStruct(got.shape, jnp.bfloat16)
    return order.call(join_kernel, "join", [shape], [VMEM_SPEC] * 2, (keep, got), us=us, behind=behind)[0]


def wait_kernel(out):
    out[...] = jnp.zeros(out.shape, out.dtype)


def wait(order, *arrays):
    order.call(wait_kernel, "wait", [jax.ShapeDtypeStruct((8, 128), jnp.float32)], [], (), us=0.5, behind=arrays)


def last_kernel(keep, got, *refs):
    *done, out = refs
    rows = keep.shape[0]
    for k, x in enumerate(done):
        out[0, pl.ds(k * rows, rows), :] = x[...]
    out[0, pl.ds(len(done) * rows, rows), :] = (keep[...] + got[...].astype(jnp.float32)).astype(jnp.bfloat16)


def pack_kernel(*refs):
    *xs, out = refs
    rows = xs[0].shape[0]
    for k, x in enumerate(xs):
        out[0, pl.ds(k * rows, rows), :] = x[...]


def whole(order, kernel, name, args, rows):
    shape = jax.ShapeDtypeStruct((1, rows, args[0].shape[1]), jnp.bfloat16)
    return order.call(kernel, name, [shape], [VMEM_SPEC] * len(args), args, vmem=8 * MIB, us=0.5)[0]


def body(act, group_of, gain, w_in, w_out):
    place = lax.axis_index("section")
    g1 = group_of[0]
    prior = route(group_of, to_next_section)[0]
    g2 = jnp.where(place == 0, 1, prior).astype(jnp.int32)
    swap = (place % Y != Y - 1).astype(jnp.int32)
    idx1, idx2 = jnp.stack([g1, swap]), jnp.stack([g2, jnp.ones((), jnp.int32)])
    order = Order()

    def across(x):
        return route(x, to_x_neighbour)

    def onward(x):
        return route(x, to_next_section)

    def mirror(*xs):
        return route(whole(order, pack_kernel, "pack", xs, len(xs) * ROWS), to_mirror)

    rows = act.shape[1]
    r_in = route(w_in, to_other_core)
    own = [act[0, : rows // 2], act[0, rows // 2 :]]
    par = [across(x) for x in own]

    r_first = route(copy_group(order, g1, w_out, 0.05), to_other_core)
    r_second = route(copy_group(order, 1 - g1, w_out, 0.05), to_other_core)
    ((w_in1, w_out1, r_in1),) = pick(order, (g1,), (w_in, w_out, r_in), us=0.1)
    hidden = up_rows(order, idx1, own[0], par[0], gain, w_in1, r_in1)
    give, keep0, r_out1 = down_load(order, idx1, own[0], par[0], hidden, w_out1, r_first, 0)
    w1 = (w_in1, w_out1, r_in1, r_out1)
    got0 = across(give)
    give, keep1 = down(order, idx1, own[0], par[0], hidden, w_out1, r_out1, ROWS, (par[1], g2.reshape(1)))
    got1 = across(give)
    give, keep2 = block(order, idx1, own[1], par[1], gain, w1, 0, 0)
    got2 = across(give)
    x0 = onward(join(order, keep0, got0))
    give, keep3 = block(order, idx1, own[1], par[1], gain, w1, ROWS, ROWS)
    got3 = across(give)
    x1 = onward(join(order, keep1, got1))
    ((w_in2, w_out2),) = pick(order, (g2,), (w_in, w_out))
    x2 = onward(join(order, keep2, got2))
    r_in2, r_out2 = load(order, g2, g2 - g1, r_in, r_first, r_second, (x0,))
    x3 = onward(join(order, keep3, got3, (x1,)))
    w2 = (w_in2, w_out2, r_in2, r_out2)

    y0, y1, y2, y3 = (across(x) for x in (x0, x1, x2, x3))
    give, keep0 = block(order, idx2, x0, y0, gain, w2, us=1)
    got0 = across(give)
    low = mirror(x0, x1)
    give, keep1 = block(order, idx2, x1, y1, gain, w2, behind=(x2,), us=1)
    got1 = across(give)
    high = mirror(x2, x3)
    give, keep2 = block(order, idx2, x2, y2, gain, w2, us=1)
    got2 = across(give)
    give, keep3 = block(order, idx2, x3, y3, gain, w2, us=1)
    got3 = across(give)
    done = [join(order, keep0, got0, us=3)]
    wait(order, low)
    done.append(join(order, keep1, got1, us=3))
    wait(order, high)
    done.append(join(order, keep2, got2, us=3))
    stash = whole(order, pack_kernel, "pack", (low[0], high[0]), rows)
    return whole(order, last_kernel, "last", (keep3, got3, *done), rows), stash


def solution(mesh):
    placed = (
        P("section", "tensor", None),
        P("section"),
        P("section", None, None),
        P("section", None, None, "tensor"),
        P("section", None, "tensor", None),
    )
    return jax.shard_map(
        body,
        mesh=mesh,
        in_specs=placed,
        out_specs=(P("section", "tensor", None), P("section", "tensor", None)),
        check_vma=False,
    )
```
